32 devices in a mesh: aux: 4 (over y, x), orb: 8 (over z, core).
Axes of the slice: x: 2, y: 2, z: 4, core: 2. Of those that a mesh axis runs over, the one named last changes fastest.
Arguments:
- integrals: bfloat16 [4096, 4, 2048], P('aux'), may hold values from -6 to 6
- int_pattern: int32 [64, 32], P('aux'), may hold values 0 or 1
- density: bfloat16 [2, 2048, 2048], P(None, 'aux', 'orb'), may hold values from -0.125 to 0.125
- dens_pattern: int32 [32, 32], P('aux', 'orb'), may hold values 0 or 1
- virt_ints: bfloat16 [2, 4096, 4, 2048], P(None, 'aux', None, 'orb'), may hold values from -0.0625 to 0.0625
Outputs:
- chi: float32 [2, 4096, 4096], P(None, 'orb', 'aux')
The draws below stay inside these ranges and needn't reach their ends.
All inputs are finite; a program needn't handle non-finite values.
Results may differ from the reference program's by a relative error of at most 0.012.
Values may be sent and summed in bfloat16 or wider, within the bound.
A program may use at most 128 MiB of HBM per device.

```python
import jax
import jax.numpy as jnp
from jax import lax

NAUX = 4096
NAO = 2048
BLK = 64
SLAB = 4
TAU = 2
N_ORB = 8


def set_ends(result, key, smallest, top_value):
    index_at = [jax.random.randint(jax.random.fold_in(key, axis), (), 0, length) for axis, length in enumerate(result.shape)]
    widest = result.shape.index(max(result.shape))
    neighbour = index_at[:widest] + [(index_at[widest] + 1) % result.shape[widest]] + index_at[widest + 1:]
    return result.at[tuple(index_at)].set(smallest).at[tuple(neighbour)].set(top_value)


def levels(own_key, extent, split, low, top_value):
    factor_of, own = 1.0, jax.random.fold_in(own_key, 6)
    for position, shards_of in split:
        draws = jnp.exp(jax.random.uniform(jax.random.fold_in(own, position), (shards_of,), jnp.float32, low / len(split), top_value / len(split)))
        factor_of = factor_of * jnp.repeat(draws, extent[position] // shards_of).reshape([-1 if axis == position else 1 for axis in range(len(extent))])
    return factor_of


def normal_values(rng, extent, width, reach, cuts=(), held_as=jnp.bfloat16):
    factor_of = levels(rng, extent, cuts, -0.22, 0.18) if cuts else 1.0
    array = jax.random.normal(rng, extent, jnp.float32) * width * factor_of
    return jnp.minimum(jnp.maximum(array, -reach), reach).astype(held_as)


def setup_inputs(seed: int = 0) -> dict:
    seeds = jax.random.split(jax.random.key(seed), 6)
    return {
        "integrals": normal_values(seeds[0], (NAUX, SLAB, NAO), 1.0, 6.0, ((0, 4),)),
        "int_pattern": set_ends((jax.random.randint(seeds[1], (NAUX // BLK, NAO // BLK), 0, 4) < 3).astype(jnp.int32), jax.random.fold_in(seeds[1], 1), 0, 1),
        "density": normal_values(seeds[2], (TAU, NAO, NAO), NAO ** -0.5, 0.125, ((1, 4), (2, 8))),
        "dens_pattern": set_ends((jax.random.randint(seeds[3], (NAO // BLK, NAO // BLK), 0, 3) < 2).astype(jnp.int32), jax.random.fold_in(seeds[3], 1), 0, 1),
        "virt_ints": normal_values(seeds[4], (TAU, NAUX, SLAB, NAO), (SLAB * NAO) ** -0.5, 0.0625, ((1, 4), (3, 8))),
    }


def expand(pattern, block_width):
    return jnp.repeat(jnp.repeat(pattern, block_width, axis=0), block_width, axis=1).astype(jnp.bfloat16)


def reference(integrals, int_pattern, density, dens_pattern, virt_ints):
    int_mask = expand(int_pattern, BLK)
    integral_rows = (integrals * int_mask[:, None, :]).reshape(NAUX * SLAB, NAO)
    dens_mask = expand(dens_pattern, BLK)
    group_width = NAO // N_ORB

    def one_moment(inputs):
        density_now, virtual_now = inputs
        occupied = jnp.dot(integral_rows, density_now * dens_mask, preferred_element_type=jnp.float32)
        occupied = occupied.astype(jnp.bfloat16).reshape(NAUX, SLAB, N_ORB, group_width)
        occ_groups = occupied.transpose(2, 0, 1, 3).reshape(N_ORB, NAUX, SLAB * group_width)
        virt_groups = virtual_now.reshape(NAUX, SLAB, N_ORB, group_width).transpose(2, 0, 1, 3).reshape(N_ORB, NAUX, SLAB * group_width)

        def add_group(total, pair):
            occ_part, virt_part = pair
            partial_value = jnp.dot(occ_part, virt_part.T, preferred_element_type=jnp.float32).astype(jnp.bfloat16)
            partial_value = lax.optimization_barrier(partial_value)
            return total + partial_value.astype(jnp.float32), None

        total, _ = lax.scan(add_group, jnp.zeros((NAUX, NAUX), jnp.float32), (occ_groups, virt_groups))
        return total

    return lax.map(one_moment, (density, virt_ints))
```

```python
import functools

import jax
import jax.numpy as jnp
from jax import lax
from jax.experimental import pallas as pl
from jax.experimental.pallas import tpu as pltpu
from jax.sharding import PartitionSpec as P

BLK = 64
CHUNKS = 16
MESH = pl.DeviceIdType.MESH


def expand(pattern, block_width):
    return jnp.repeat(jnp.repeat(pattern, block_width, axis=0), block_width, axis=1).astype(
        jnp.bfloat16
    )


def ring_kernel(chunks, ints, d_own, d_sib, v_own, v_sib, out, occ, psum, zrecv, ibuf, isem, xs, xr, zs, zr):
    slab, rows = ibuf.shape[1], ibuf.shape[2]
    per_moment = out.shape[1] // rows
    cols = d_own.shape[2]
    width = slab * cols
    half = rows // 2
    a = lax.axis_index("aux")
    o = lax.axis_index("orb")
    z = o // 2
    ax = a + 1 - 2 * (a % 2)
    ay = (a + 2) % 4
    ad = 3 - a

    def rcopy(src, dst, send, recv, dev):
        return pltpu.make_async_remote_copy(
            src_ref=src, dst_ref=dst, send_sem=send, recv_sem=recv, device_id=dev, device_id_type=MESH
        )

    def own(i, kind, slot):
        ref = occ.at[slot, i]
        return rcopy(ref, ref, xs.at[kind, i], xr.at[kind, i], (ax if kind == 0 else ay, o))

    def forward(i, kind, slot):
        ref = occ.at[slot, i, pl.ds(0 if kind == 2 else half, half)]
        return rcopy(ref, ref, xs.at[kind, i], xr.at[kind, i], (ay if kind == 2 else ax, o))

    def up(i, frm, at_end):
        low = frm + 1
        src = psum.at[i, pl.ds(low, 4 - low)] if at_end else zrecv.at[i, pl.ds(low + 1, 4 - low)]
        return rcopy(src, zrecv.at[i, pl.ds(low + 1, 4 - low)], zs.at[0, i], zr.at[0, i], (a, 2 * (frm + 1) + o % 2))

    def down(i, frm, at_end):
        src = psum.at[i, pl.ds(0, frm)] if at_end else zrecv.at[i, pl.ds(0, frm)]
        return rcopy(src, zrecv.at[i, pl.ds(0, frm)], zs.at[1, i], zr.at[1, i], (a, 2 * (frm - 1) + o % 2))

    def fetch(i):
        return pltpu.make_async_copy(
            ints.at[:, pl.ds((i % per_moment) * rows, rows), :], ibuf.at[i % 2], isem.at[i % 2]
        )

    fetch(0).start()

    barrier = pltpu.get_barrier_semaphore()
    pl.semaphore_signal(barrier, inc=1, device_id=(ax, o), device_id_type=MESH)
    pl.semaphore_signal(barrier, inc=1, device_id=(ay, o), device_id_type=MESH)

    @pl.when(z > 0)
    def _():
        pl.semaphore_signal(barrier, inc=1, device_id=(a, o - 2), device_id_type=MESH)

    @pl.when(z < 3)
    def _():
        pl.semaphore_signal(barrier, inc=1, device_id=(a, o + 2), device_id_type=MESH)

    inner = (z > 0) & (z < 3)

    @pl.when(inner)
    def _():
        pl.semaphore_wait(barrier, 4)

    @pl.when(jnp.logical_not(inner))
    def _():
        pl.semaphore_wait(barrier, 3)

    def make(i):
        fetch(i).wait()

        @pl.when(i + 1 < chunks)
        def _():
            fetch(i + 1).start()

        t = i // per_moment
        x = ibuf[i % 2].reshape(slab * rows, ibuf.shape[3])
        for base, dens in ((0, d_own), (width, d_sib)):
            y = jnp.dot(x, dens[t], preferred_element_type=jnp.float32).astype(jnp.bfloat16)
            for s in range(slab):
                occ[a, i, :, base + s * cols : base + (s + 1) * cols] = y[s * rows : (s + 1) * rows]
        own(i, 0, a).start()
        own(i, 1, a).start()

    def relay(i):
        own(i, 0, ax).wait_recv()
        forward(i, 2, ax).start()
        own(i, 1, ay).wait_recv()
        forward(i, 3, ay).start()

    def multiply(i):
        forward(i, 2, ad).wait_recv()
        forward(i, 3, ad).wait_recv()
        t = i // per_moment
        for d in range(0, 4, 2):
            left = occ[d : d + 2, i].reshape(2 * rows, 2 * width)
            p = jnp.dot(left[:, :width], v_own[t], preferred_element_type=jnp.float32)
            p += jnp.dot(left[:, width:], v_sib[t], preferred_element_type=jnp.float32)
            psum[i, d : d + 2] = p.astype(jnp.bfloat16).reshape(2, rows, psum.shape[3])

        @pl.when(z == 0)
        def _():
            up(i, 0, True).start()

        @pl.when(z == 3)
        def _():
            down(i, 3, True).start()

    def add(i, slot, d):
        total = zrecv[i, slot].astype(jnp.float32) + psum[i, d].astype(jnp.float32)
        zrecv[i, slot] = total.astype(jnp.bfloat16)

    def hop1(i):
        @pl.when(z == 1)
        def _():
            up(i, 0, True).wait_recv()
            for d in (2, 3):
                add(i, d + 1, d)
            up(i, 1, False).start()

        @pl.when(z == 2)
        def _():
            down(i, 3, True).wait_recv()
            for d in (0, 1):
                add(i, d, d)
            down(i, 2, False).start()

    def hop2(i):
        @pl.when(z == 2)
        def _():
            up(i, 1, False).wait_recv()
            add(i, 4, 3)
            up(i, 2, False).start()

        @pl.when(z == 1)
        def _():
            down(i, 2, False).wait_recv()
            add(i, 0, 0)
            down(i, 1, False).start()

    def finish(i):
        where = pl.ds((i % per_moment) * rows, rows)
        t = i // per_moment

        @pl.when(z == 0)
        def _():
            down(i, 1, False).wait_recv()
            out[t, where] = psum[i, 0].astype(jnp.float32) + zrecv[i, 0].astype(jnp.float32)

        @pl.when(z == 3)
        def _():
            up(i, 2, False).wait_recv()
            out[t, where] = psum[i, 3].astype(jnp.float32) + zrecv[i, 4].astype(jnp.float32)

        @pl.when(inner)
        def _():
            total = zrecv[i, z].astype(jnp.float32) + zrecv[i, z + 1].astype(jnp.float32)
            out[t, where] = total + psum[i, z].astype(jnp.float32)

    stages = ((make, 0), (relay, 2), (multiply, 3), (hop1, 4), (hop2, 5), (finish, 6))

    @pl.loop(0, chunks + stages[-1][1])
    def _(step):
        for stage, lag in stages:

            @pl.when((step >= lag) & (step < chunks + lag))
            def _(stage=stage, lag=lag):
                stage(step - lag)

    @pl.loop(0, chunks)
    def _(i):
        own(i, 0, a).wait_send()
        own(i, 1, a).wait_send()
        forward(i, 2, ax).wait_send()
        forward(i, 3, ay).wait_send()
        for place in range(4):

            @pl.when(z == place)
            def _(place=place):
                if place < 3:
                    up(i, place, place == 0).wait_send()
                if place > 0:
                    down(i, place, place == 3).wait_send()


def on_grid(integrals, int_pattern, density, dens_pattern, virt_ints):
    aux_rows, slab, orbitals = integrals.shape
    times, _, cols = density.shape
    core = lax.axis_index("orb") % 2
    mine = aux_rows // 2
    pairs = [(i, i + 1 - 2 * (i % 2)) for i in range(8)]
    v_other = lax.ppermute(virt_ints, "orb", pairs)
    masked_density = density * expand(dens_pattern, BLK)[None]
    d_own = lax.all_gather(masked_density, "aux", axis=1, tiled=True)
    d_sib = lax.ppermute(d_own, "orb", pairs)
    picked = lax.dynamic_slice_in_dim(integrals, core * mine, mine, 0)
    pattern = lax.dynamic_slice_in_dim(int_pattern, core * (mine // BLK), mine // BLK, 0)
    ints = jnp.transpose(picked * expand(pattern, BLK)[:, None, :], (1, 0, 2))

    def turned(v):
        return jnp.transpose(v, (0, 2, 3, 1)).reshape(times, slab * cols, aux_rows)

    rows = times * mine // CHUNKS
    width = slab * cols
    bf16 = jnp.bfloat16
    vmem = pl.BlockSpec(memory_space=pltpu.VMEM)
    return pl.pallas_call(
        functools.partial(ring_kernel, CHUNKS),
        out_shape=jax.ShapeDtypeStruct((times, mine, aux_rows), jnp.float32),
        in_specs=[pl.BlockSpec(memory_space=pl.ANY), vmem, vmem, vmem, vmem],
        out_specs=vmem,
        scratch_shapes=[
            pltpu.VMEM((4, CHUNKS, rows, 2 * width), bf16),
            pltpu.VMEM((CHUNKS, 4, rows, aux_rows), bf16),
            pltpu.VMEM((CHUNKS, 5, rows, aux_rows), bf16),
            pltpu.VMEM((2, slab, rows, orbitals), bf16),
            pltpu.SemaphoreType.DMA((2,)),
            pltpu.SemaphoreType.DMA((4, CHUNKS)),
            pltpu.SemaphoreType.DMA((4, CHUNKS)),
            pltpu.SemaphoreType.DMA((2, CHUNKS)),
            pltpu.SemaphoreType.DMA((2, CHUNKS)),
        ],
        compiler_params=pltpu.CompilerParams(
            collective_id=0, has_side_effects=True, vmem_limit_bytes=60 * 1024 * 1024
        ),
        cost_estimate=pl.CostEstimate(
            flops=2 * times * slab * aux_rows * cols * (orbitals + 4 * aux_rows),
            bytes_accessed=64 << 20,
            transcendentals=0,
        ),
    )(ints, d_own, d_sib, turned(virt_ints), turned(v_other))


def on_device(integrals, int_pattern, density, dens_pattern, virt_ints):
    aux_rows, slab_width, orbitals = integrals.shape
    times_count, _, columns = density.shape
    int_mask = expand(int_pattern, BLK)
    integral_rows = (integrals * int_mask[:, None, :]).reshape(aux_rows * slab_width, orbitals)
    masked_density = density * expand(dens_pattern, BLK)[None]
    occupied_list = []
    for moment in range(times_count):
        occupied_list.append(
            jnp.dot(
                integral_rows,
                lax.all_gather(masked_density[moment], "aux", axis=0, tiled=True),
                preferred_element_type=jnp.float32,
            )
        )
    occupied = jnp.stack(occupied_list)
    occupied = occupied.astype(jnp.bfloat16).reshape(times_count, aux_rows, slab_width * columns)
    virtual_rows = virt_ints.reshape(times_count, virt_ints.shape[1], slab_width * columns)
    partial_chi = jnp.einsum(
        "tpk,tqk->tpq",
        lax.all_gather(occupied, "aux", axis=1, tiled=True),
        virtual_rows,
        preferred_element_type=jnp.float32,
    )
    return lax.psum_scatter(
        partial_chi.astype(jnp.bfloat16), "orb", scatter_dimension=1, tiled=True
    ).astype(jnp.float32)


def solution(mesh):
    in_specs = (
        P("aux", None, None),
        P("aux", None),
        P(None, "aux", "orb"),
        P("aux", "orb"),
        P(None, "aux", None, "orb"),
    )
    out_specs = P(None, "orb", "aux")
    small = mesh.shape["aux"] == 4 and mesh.shape["orb"] == 8
    return jax.shard_map(
        on_grid if small else on_device,
        mesh=mesh,
        in_specs=in_specs,
        out_specs=out_specs,
        check_vma=False,
    )
```

```python
import functools

import jax
import jax.numpy as jnp
from jax import lax
from jax.experimental import pallas as pl
from jax.experimental.pallas import tpu as pltpu
from jax.sharding import PartitionSpec as P

BLK = 64
CHUNKS = 16
MESH = pl.DeviceIdType.MESH


def expand(pattern, block_width):
    return jnp.repeat(jnp.repeat(pattern, block_width, axis=0), block_width, axis=1).astype(
        jnp.bfloat16
    )


def ring_kernel(
    chunks, ints, mask, dens, virt, out, occ, psum, zrecv, ibuf, ybuf, dall, vall,
    isem, xs, xr, zs, zr, dl, ds, dr, es, er, vl, vs, vr,
):
    rows, slab = ibuf.shape[1], ibuf.shape[2]
    per_moment = out.shape[1] // rows
    cols = dens.shape[2]
    width = slab * cols
    half = rows // 2
    a = lax.axis_index("aux")
    o = lax.axis_index("orb")
    z = o // 2
    ax = a + 1 - 2 * (a % 2)
    ay = (a + 2) % 4
    ad = 3 - a
    core = o % 2
    sib = o + 1 - 2 * core
    depth = dens.shape[1]

    def rcopy(src, dst, send, recv, dev):
        return pltpu.make_async_remote_copy(
            src_ref=src, dst_ref=dst, send_sem=send, recv_sem=recv, device_id=dev, device_id_type=MESH
        )

    def own(i, kind, slot):
        ref = occ.at[slot, i]
        return rcopy(ref, ref, xs.at[kind, i], xr.at[kind, i], (ax if kind == 0 else ay, o))

    def forward(i, kind, slot):
        ref = occ.at[slot, i, pl.ds(0 if kind == 2 else half, half)]
        return rcopy(ref, ref, xs.at[kind, i], xr.at[kind, i], (ay if kind == 2 else ax, o))

    def up(i, frm, at_end):
        low = frm + 1
        src = psum.at[i, pl.ds(low, 4 - low)] if at_end else zrecv.at[i, pl.ds(low + 1, 4 - low)]
        return rcopy(src, zrecv.at[i, pl.ds(low + 1, 4 - low)], zs.at[0, i], zr.at[0, i], (a, 2 * (frm + 1) + o % 2))

    def down(i, frm, at_end):
        src = psum.at[i, pl.ds(0, frm)] if at_end else zrecv.at[i, pl.ds(0, frm)]
        return rcopy(src, zrecv.at[i, pl.ds(0, frm)], zs.at[1, i], zr.at[1, i], (a, 2 * (frm - 1) + o % 2))

    def fetch(i):
        return pltpu.make_async_copy(
            ints.at[pl.ds(core * out.shape[1] + (i % per_moment) * rows, rows)], ibuf.at[i % 2], isem.at[i % 2]
        )

    def d_local(t):
        return pltpu.make_async_copy(dens.at[t], dall.at[0, t, a], dl.at[t])

    def d_own(t, kind):
        return rcopy(
            dens.at[t], dall.at[0, t, a], ds.at[kind, t], dr.at[kind, t], (ax if kind == 0 else ay, o)
        )

    def d_forward(t, kind, slot):
        part = pl.ds(0 if kind == 2 else depth // 2, depth // 2)
        ref = dall.at[0, t, slot, part]
        return rcopy(ref, ref, ds.at[kind, t], dr.at[kind, t], (ay if kind == 2 else ax, o))

    def d_cross(t, kind, slot):
        src = dens.at[t] if kind == 0 else dall.at[0, t, slot]
        return rcopy(src, dall.at[1, t, slot], es.at[kind, t], er.at[kind, t], (a, sib))

    def v_local(t):
        return pltpu.make_async_copy(virt.at[t], vall.at[0, t], vl.at[t])

    def v_cross(t):
        return rcopy(virt.at[t], vall.at[1, t], vs.at[t], vr.at[t], (a, sib))

    fetch(0).start()
    d_local(0).start()
    v_local(0).start()
    d_local(1).start()
    v_local(1).start()

    barrier = pltpu.get_barrier_semaphore()
    pl.semaphore_signal(barrier, inc=1, device_id=(ax, o), device_id_type=MESH)
    pl.semaphore_signal(barrier, inc=1, device_id=(ay, o), device_id_type=MESH)
    pl.semaphore_signal(barrier, inc=1, device_id=(a, sib), device_id_type=MESH)

    @pl.when(z > 0)
    def _():
        pl.semaphore_signal(barrier, inc=1, device_id=(a, o - 2), device_id_type=MESH)

    @pl.when(z < 3)
    def _():
        pl.semaphore_signal(barrier, inc=1, device_id=(a, o + 2), device_id_type=MESH)

    inner = (z > 0) & (z < 3)

    @pl.when(inner)
    def _():
        pl.semaphore_wait(barrier, 5)

    @pl.when(jnp.logical_not(inner))
    def _():
        pl.semaphore_wait(barrier, 4)

    def d_send(t):
        d_own(t, 0).start()
        d_own(t, 1).start()
        d_cross(t, 0, a).start()
        v_cross(t).start()

    def d_relay(t):
        d_own(t, 0).wait_recv()
        d_forward(t, 2, ax).start()
        d_cross(t, 1, ax).start()
        d_own(t, 1).wait_recv()
        d_forward(t, 3, ay).start()
        d_cross(t, 2, ay).start()

    def d_finish(t):
        d_forward(t, 2, ad).wait_recv()
        d_forward(t, 3, ad).wait_recv()
        d_cross(t, 3, ad).start()
        d_local(t).wait()
        for kind, slot in enumerate((a, ax, ay, ad)):
            d_cross(t, kind, slot).wait_recv()

    d_send(0)
    d_relay(0)
    d_finish(0)

    def make(i):
        fetch(i).wait()

        @pl.when(i + 1 < chunks)
        def _():
            fetch(i + 1).start()

        t = i // per_moment
        x = (ibuf[i % 2] * mask[i % per_moment][None]).reshape(rows * slab, ibuf.shape[3])
        for side in range(2):
            d = dall[side, t].reshape(4 * depth, cols)
            y = jnp.dot(x, d, preferred_element_type=jnp.float32)
            for part in range(cols // 128):
                ybuf[part] = y[:, part * 128 : (part + 1) * 128]
            for s in range(slab):
                base = side * width + s * cols
                for part in range(cols // 128):
                    piece = ybuf[part, pl.ds(s, rows, stride=slab), :]
                    low = base + part * 128
                    occ[a, i, :, low : low + 128] = piece.astype(jnp.bfloat16)
        own(i, 0, a).start()
        own(i, 1, a).start()

    def relay(i):
        own(i, 0, ax).wait_recv()
        forward(i, 2, ax).start()
        own(i, 1, ay).wait_recv()
        forward(i, 3, ay).start()

    def multiply(i):
        forward(i, 2, ad).wait_recv()
        forward(i, 3, ad).wait_recv()
        t = i // per_moment

        @pl.when(i % per_moment == 0)
        def _():
            v_local(t).wait()
            v_cross(t).wait_recv()

        for d in range(0, 4, 2):
            left = occ[d : d + 2, i].reshape(2 * rows, 2 * width)
            p = jnp.dot(left[:, :width], vall[0, t], preferred_element_type=jnp.float32)
            p += jnp.dot(left[:, width:], vall[1, t], preferred_element_type=jnp.float32)
            psum[i, d : d + 2] = p.astype(jnp.bfloat16).reshape(2, rows, psum.shape[3])

        @pl.when(z == 0)
        def _():
            up(i, 0, True).start()

        @pl.when(z == 3)
        def _():
            down(i, 3, True).start()

    def add(i, slot, d):
        total = zrecv[i, slot].astype(jnp.float32) + psum[i, d].astype(jnp.float32)
        zrecv[i, slot] = total.astype(jnp.bfloat16)

    def hop1(i):
        @pl.when(z == 1)
        def _():
            up(i, 0, True).wait_recv()
            for d in (2, 3):
                add(i, d + 1, d)
            up(i, 1, False).start()

        @pl.when(z == 2)
        def _():
            down(i, 3, True).wait_recv()
            for d in (0, 1):
                add(i, d, d)
            down(i, 2, False).start()

    def hop2(i):
        @pl.when(z == 2)
        def _():
            up(i, 1, False).wait_recv()
            add(i, 4, 3)
            up(i, 2, False).start()

        @pl.when(z == 1)
        def _():
            down(i, 2, False).wait_recv()
            add(i, 0, 0)
            down(i, 1, False).start()

    def finish(i):
        where = pl.ds((i % per_moment) * rows, rows)
        t = i // per_moment

        @pl.when(z == 0)
        def _():
            down(i, 1, False).wait_recv()
            out[t, where] = psum[i, 0].astype(jnp.float32) + zrecv[i, 0].astype(jnp.float32)

        @pl.when(z == 3)
        def _():
            up(i, 2, False).wait_recv()
            out[t, where] = psum[i, 3].astype(jnp.float32) + zrecv[i, 4].astype(jnp.float32)

        @pl.when(inner)
        def _():
            total = zrecv[i, z].astype(jnp.float32) + zrecv[i, z + 1].astype(jnp.float32)
            out[t, where] = total + psum[i, z].astype(jnp.float32)

    stages = ((make, 0), (relay, 2), (multiply, 3), (hop1, 4), (hop2, 5), (finish, 6))

    @pl.loop(0, chunks + stages[-1][1])
    def _(step):
        for stage, lag in stages:

            @pl.when((step >= lag) & (step < chunks + lag))
            def _(stage=stage, lag=lag):
                stage(step - lag)

        for at, part in ((1, d_send), (3, d_relay), (5, d_finish)):

            @pl.when(step == at)
            def _(part=part):
                part(1)

    for t in range(2):
        for kind in range(2):
            d_own(t, kind).wait_send()
        d_forward(t, 2, ax).wait_send()
        d_forward(t, 3, ay).wait_send()
        for kind, slot in enumerate((a, ax, ay, ad)):
            d_cross(t, kind, slot).wait_send()
        v_cross(t).wait_send()

    @pl.loop(0, chunks)
    def _(i):
        own(i, 0, a).wait_send()
        own(i, 1, a).wait_send()
        forward(i, 2, ax).wait_send()
        forward(i, 3, ay).wait_send()
        for place in range(4):

            @pl.when(z == place)
            def _(place=place):
                if place < 3:
                    up(i, place, place == 0).wait_send()
                if place > 0:
                    down(i, place, place == 3).wait_send()


def on_grid(integrals, int_pattern, density, dens_pattern, virt_ints):
    aux_rows, slab, orbitals = integrals.shape
    times, _, cols = density.shape
    core = lax.axis_index("orb") % 2
    mine = aux_rows // 2
    masked_density = density * expand(dens_pattern, BLK)[None]
    pattern = lax.dynamic_slice_in_dim(int_pattern, core * (mine // BLK), mine // BLK, 0)
    rows = times * mine // CHUNKS
    mask = jnp.repeat(pattern, BLK, axis=1).astype(jnp.bfloat16)
    mask = jnp.repeat(mask, BLK // rows, axis=0)[:, None, :]

    def turned(v):
        return jnp.transpose(v, (0, 2, 3, 1)).reshape(times, slab * cols, aux_rows)

    width = slab * cols
    bf16 = jnp.bfloat16
    hbm = pl.BlockSpec(memory_space=pl.ANY)
    vmem = pl.BlockSpec(memory_space=pltpu.VMEM)
    return pl.pallas_call(
        functools.partial(ring_kernel, CHUNKS),
        out_shape=jax.ShapeDtypeStruct((times, mine, aux_rows), jnp.float32),
        in_specs=[hbm, vmem, vmem, hbm],
        out_specs=vmem,
        scratch_shapes=[
            pltpu.VMEM((4, CHUNKS, rows, 2 * width), bf16),
            pltpu.VMEM((CHUNKS, 4, rows, aux_rows), bf16),
            pltpu.VMEM((CHUNKS, 5, rows, aux_rows), bf16),
            pltpu.VMEM((2, rows, slab, orbitals), bf16),
            pltpu.VMEM((cols // 128, rows * slab, 128), jnp.float32),
            pltpu.VMEM((2, times, 4, orbitals // 4, cols), bf16),
            pltpu.VMEM((2, times, width, aux_rows), bf16),
            pltpu.SemaphoreType.DMA((2,)),
            pltpu.SemaphoreType.DMA((4, CHUNKS)),
            pltpu.SemaphoreType.DMA((4, CHUNKS)),
            pltpu.SemaphoreType.DMA((2, CHUNKS)),
            pltpu.SemaphoreType.DMA((2, CHUNKS)),
            pltpu.SemaphoreType.DMA((2,)),
            pltpu.SemaphoreType.DMA((4, 2)),
            pltpu.SemaphoreType.DMA((4, 2)),
            pltpu.SemaphoreType.DMA((4, 2)),
            pltpu.SemaphoreType.DMA((4, 2)),
            pltpu.SemaphoreType.DMA((2,)),
            pltpu.SemaphoreType.DMA((2,)),
            pltpu.SemaphoreType.DMA((2,)),
        ],
        compiler_params=pltpu.CompilerParams(
            collective_id=0, has_side_effects=True, vmem_limit_bytes=60 * 1024 * 1024
        ),
        cost_estimate=pl.CostEstimate(
            flops=2 * times * slab * aux_rows * cols * (orbitals + 4 * aux_rows),
            bytes_accessed=64 << 20,
            transcendentals=0,
        ),
    )(integrals, mask, masked_density, turned(virt_ints))


def on_device(integrals, int_pattern, density, dens_pattern, virt_ints):
    aux_rows, slab_width, orbitals = integrals.shape
    times_count, _, columns = density.shape
    int_mask = expand(int_pattern, BLK)
    integral_rows = (integrals * int_mask[:, None, :]).reshape(aux_rows * slab_width, orbitals)
    masked_density = density * expand(dens_pattern, BLK)[None]
    occupied_list = []
    for moment in range(times_count):
        occupied_list.append(
            jnp.dot(
                integral_rows,
                lax.all_gather(masked_density[moment], "aux", axis=0, tiled=True),
                preferred_element_type=jnp.float32,
            )
        )
    occupied = jnp.stack(occupied_list)
    occupied = occupied.astype(jnp.bfloat16).reshape(times_count, aux_rows, slab_width * columns)
    virtual_rows = virt_ints.reshape(times_count, virt_ints.shape[1], slab_width * columns)
    partial_chi = jnp.einsum(
        "tpk,tqk->tpq",
        lax.all_gather(occupied, "aux", axis=1, tiled=True),
        virtual_rows,
        preferred_element_type=jnp.float32,
    )
    return lax.psum_scatter(
        partial_chi.astype(jnp.bfloat16), "orb", scatter_dimension=1, tiled=True
    ).astype(jnp.float32)


def solution(mesh):
    in_specs = (
        P("aux", None, None),
        P("aux", None),
        P(None, "aux", "orb"),
        P("aux", "orb"),
        P(None, "aux", None, "orb"),
    )
    out_specs = P(None, "orb", "aux")
    small = mesh.shape["aux"] == 4 and mesh.shape["orb"] == 8
    return jax.shard_map(
        on_grid if small else on_device,
        mesh=mesh,
        in_specs=in_specs,
        out_specs=out_specs,
        check_vma=False,
    )
```

```python
import functools

import jax
import jax.numpy as jnp
from jax import lax
from jax.experimental import pallas as pl
from jax.experimental.pallas import tpu as pltpu
from jax.sharding import PartitionSpec as P

BLK = 64
CHUNKS = 32
MESH = pl.DeviceIdType.MESH


def expand(pattern, block_width):
    return jnp.repeat(jnp.repeat(pattern, block_width, axis=0), block_width, axis=1).astype(
        jnp.bfloat16
    )


def ring_kernel(
    chunks, ints, mask, dens, virt, out, occ, psum, zrecv, ibuf, ybuf, dall, vall,
    isem, xs, xr, zs, zr, dl, ds, dr, es, er, vl, vs, vr,
):
    rows, slab = ibuf.shape[1], ibuf.shape[2]
    per_moment = out.shape[1] // rows
    cols = dens.shape[2]
    width = slab * cols
    half = rows // 2
    a = lax.axis_index("aux")
    o = lax.axis_index("orb")
    z = o // 2
    ax = a + 1 - 2 * (a % 2)
    ay = (a + 2) % 4
    ad = 3 - a
    core = o % 2
    sib = o + 1 - 2 * core
    depth = dens.shape[1]

    def rcopy(src, dst, send, recv, dev):
        return pltpu.make_async_remote_copy(
            src_ref=src, dst_ref=dst, send_sem=send, recv_sem=recv, device_id=dev, device_id_type=MESH
        )

    def own(i, kind, slot):
        ref = occ.at[slot, i]
        return rcopy(ref, ref, xs.at[kind, i], xr.at[kind, i], (ax if kind == 0 else ay, o))

    def forward(i, kind, slot):
        ref = occ.at[slot, i, pl.ds(0 if kind == 2 else half, half)]
        return rcopy(ref, ref, xs.at[kind, i], xr.at[kind, i], (ay if kind == 2 else ax, o))

    def up(i, frm, at_end):
        low = frm + 1
        src = psum.at[i, pl.ds(low, 4 - low)] if at_end else zrecv.at[i, pl.ds(low + 1, 4 - low)]
        return rcopy(src, zrecv.at[i, pl.ds(low + 1, 4 - low)], zs.at[0, i], zr.at[0, i], (a, 2 * (frm + 1) + o % 2))

    def down(i, frm, at_end):
        src = psum.at[i, pl.ds(0, frm)] if at_end else zrecv.at[i, pl.ds(0, frm)]
        return rcopy(src, zrecv.at[i, pl.ds(0, frm)], zs.at[1, i], zr.at[1, i], (a, 2 * (frm - 1) + o % 2))

    def fetch(i):
        return pltpu.make_async_copy(
            ints.at[pl.ds(core * out.shape[1] + (i % per_moment) * rows, rows)], ibuf.at[i % 2], isem.at[i % 2]
        )

    def d_local(t):
        return pltpu.make_async_copy(dens.at[t], dall.at[0, t, a], dl.at[t])

    def d_own(t, kind):
        return rcopy(
            dens.at[t], dall.at[0, t, a], ds.at[kind, t], dr.at[kind, t], (ax if kind == 0 else ay, o)
        )

    def d_forward(t, kind, slot):
        part = pl.ds(0 if kind == 2 else depth // 2, depth // 2)
        ref = dall.at[0, t, slot, part]
        return rcopy(ref, ref, ds.at[kind, t], dr.at[kind, t], (ay if kind == 2 else ax, o))

    def d_cross(t, kind, slot):
        src = dens.at[t] if kind == 0 else dall.at[0, t, slot]
        return rcopy(src, dall.at[1, t, slot], es.at[kind, t], er.at[kind, t], (a, sib))

    def v_local(t):
        return pltpu.make_async_copy(virt.at[t], vall.at[0, t], vl.at[t])

    def v_cross(t):
        return rcopy(virt.at[t], vall.at[1, t], vs.at[t], vr.at[t], (a, sib))

    fetch(0).start()
    d_local(0).start()
    v_local(0).start()
    d_local(1).start()
    v_local(1).start()

    barrier = pltpu.get_barrier_semaphore()
    pl.semaphore_signal(barrier, inc=1, device_id=(ax, o), device_id_type=MESH)
    pl.semaphore_signal(barrier, inc=1, device_id=(ay, o), device_id_type=MESH)
    pl.semaphore_signal(barrier, inc=1, device_id=(a, sib), device_id_type=MESH)

    @pl.when(z > 0)
    def _():
        pl.semaphore_signal(barrier, inc=1, device_id=(a, o - 2), device_id_type=MESH)

    @pl.when(z < 3)
    def _():
        pl.semaphore_signal(barrier, inc=1, device_id=(a, o + 2), device_id_type=MESH)

    inner = (z > 0) & (z < 3)

    @pl.when(inner)
    def _():
        pl.semaphore_wait(barrier, 5)

    @pl.when(jnp.logical_not(inner))
    def _():
        pl.semaphore_wait(barrier, 4)

    def d_send(t):
        d_own(t, 0).start()
        d_own(t, 1).start()
        d_cross(t, 0, a).start()
        v_cross(t).start()

    def d_relay(t):
        d_own(t, 0).wait_recv()
        d_forward(t, 2, ax).start()
        d_cross(t, 1, ax).start()
        d_own(t, 1).wait_recv()
        d_forward(t, 3, ay).start()
        d_cross(t, 2, ay).start()

    def d_finish(t):
        d_forward(t, 2, ad).wait_recv()
        d_forward(t, 3, ad).wait_recv()
        d_cross(t, 3, ad).start()
        d_local(t).wait()
        for kind, slot in enumerate((a, ax, ay, ad)):
            d_cross(t, kind, slot).wait_recv()

    d_send(0)
    d_relay(0)
    d_finish(0)

    def make(i):
        fetch(i).wait()

        @pl.when(i + 1 < chunks)
        def _():
            fetch(i + 1).start()

        t = i // per_moment
        x = (ibuf[i % 2] * mask[i % per_moment][None]).reshape(rows * slab, ibuf.shape[3])
        for side in range(2):
            d = dall[side, t].reshape(4 * depth, cols)
            y = jnp.dot(x, d, preferred_element_type=jnp.float32)
            for part in range(cols // 128):
                ybuf[part] = y[:, part * 128 : (part + 1) * 128]
            for s in range(slab):
                base = side * width + s * cols
                for part in range(cols // 128):
                    piece = ybuf[part, pl.ds(s, rows, stride=slab), :]
                    low = base + part * 128
                    occ[a, i, :, low : low + 128] = piece.astype(jnp.bfloat16)
        own(i, 0, a).start()
        own(i, 1, a).start()

    def relay(i):
        own(i, 0, ax).wait_recv()
        forward(i, 2, ax).start()
        own(i, 1, ay).wait_recv()
        forward(i, 3, ay).start()

    def multiply(i):
        forward(i, 2, ad).wait_recv()
        forward(i, 3, ad).wait_recv()
        t = i // per_moment

        @pl.when(i % per_moment == 0)
        def _():
            v_local(t).wait()
            v_cross(t).wait_recv()

        for d in range(0, 4, 2):
            left = occ[d : d + 2, i].reshape(2 * rows, 2 * width)
            p = jnp.dot(left[:, :width], vall[0, t], preferred_element_type=jnp.float32)
            p += jnp.dot(left[:, width:], vall[1, t], preferred_element_type=jnp.float32)
            psum[i, d : d + 2] = p.astype(jnp.bfloat16).reshape(2, rows, psum.shape[3])

        @pl.when(z == 0)
        def _():
            up(i, 0, True).start()

        @pl.when(z == 3)
        def _():
            down(i, 3, True).start()

    def add(i, slot, d):
        total = zrecv[i, slot].astype(jnp.float32) + psum[i, d].astype(jnp.float32)
        zrecv[i, slot] = total.astype(jnp.bfloat16)

    def hop1(i):
        @pl.when(z == 1)
        def _():
            up(i, 0, True).wait_recv()
            for d in (2, 3):
                add(i, d + 1, d)
            up(i, 1, False).start()

        @pl.when(z == 2)
        def _():
            down(i, 3, True).wait_recv()
            for d in (0, 1):
                add(i, d, d)
            down(i, 2, False).start()

    def hop2(i):
        @pl.when(z == 2)
        def _():
            up(i, 1, False).wait_recv()
            add(i, 4, 3)
            up(i, 2, False).start()

        @pl.when(z == 1)
        def _():
            down(i, 2, False).wait_recv()
            add(i, 0, 0)
            down(i, 1, False).start()

    def finish(i):
        where = pl.ds((i % per_moment) * rows, rows)
        t = i // per_moment

        @pl.when(z == 0)
        def _():
            down(i, 1, False).wait_recv()
            out[t, where] = psum[i, 0].astype(jnp.float32) + zrecv[i, 0].astype(jnp.float32)

        @pl.when(z == 3)
        def _():
            up(i, 2, False).wait_recv()
            out[t, where] = psum[i, 3].astype(jnp.float32) + zrecv[i, 4].astype(jnp.float32)

        @pl.when(inner)
        def _():
            total = zrecv[i, z].astype(jnp.float32) + zrecv[i, z + 1].astype(jnp.float32)
            out[t, where] = total + psum[i, z].astype(jnp.float32)

    stages = ((relay, 2), (make, 0), (multiply, 4), (hop1, 6), (hop2, 8), (finish, 10))

    @pl.loop(0, chunks + stages[-1][1])
    def _(step):
        for stage, lag in stages:

            @pl.when((step >= lag) & (step < chunks + lag))
            def _(stage=stage, lag=lag):
                stage(step - lag)

        for at, part in ((1, d_send), (3, d_relay), (5, d_finish)):

            @pl.when(step == at)
            def _(part=part):
                part(1)

    for t in range(2):
        for kind in range(2):
            d_own(t, kind).wait_send()
        d_forward(t, 2, ax).wait_send()
        d_forward(t, 3, ay).wait_send()
        for kind, slot in enumerate((a, ax, ay, ad)):
            d_cross(t, kind, slot).wait_send()
        v_cross(t).wait_send()

    @pl.loop(0, chunks)
    def _(i):
        own(i, 0, a).wait_send()
        own(i, 1, a).wait_send()
        forward(i, 2, ax).wait_send()
        forward(i, 3, ay).wait_send()
        for place in range(4):

            @pl.when(z == place)
            def _(place=place):
                if place < 3:
                    up(i, place, place == 0).wait_send()
                if place > 0:
                    down(i, place, place == 3).wait_send()


def on_grid(integrals, int_pattern, density, dens_pattern, virt_ints):
    aux_rows, slab, orbitals = integrals.shape
    times, _, cols = density.shape
    core = lax.axis_index("orb") % 2
    mine = aux_rows // 2
    masked_density = density * expand(dens_pattern, BLK)[None]
    pattern = lax.dynamic_slice_in_dim(int_pattern, core * (mine // BLK), mine // BLK, 0)
    rows = times * mine // CHUNKS
    mask = jnp.repeat(pattern, BLK, axis=1).astype(jnp.bfloat16)
    mask = jnp.repeat(mask, BLK // rows, axis=0)[:, None, :]

    def turned(v):
        return jnp.transpose(v, (0, 2, 3, 1)).reshape(times, slab * cols, aux_rows)

    width = slab * cols
    bf16 = jnp.bfloat16
    hbm = pl.BlockSpec(memory_space=pl.ANY)
    vmem = pl.BlockSpec(memory_space=pltpu.VMEM)
    return pl.pallas_call(
        functools.partial(ring_kernel, CHUNKS),
        out_shape=jax.ShapeDtypeStruct((times, mine, aux_rows), jnp.float32),
        in_specs=[hbm, vmem, vmem, hbm],
        out_specs=vmem,
        scratch_shapes=[
            pltpu.VMEM((4, CHUNKS, rows, 2 * width), bf16),
            pltpu.VMEM((CHUNKS, 4, rows, aux_rows), bf16),
            pltpu.VMEM((CHUNKS, 5, rows, aux_rows), bf16),
            pltpu.VMEM((2, rows, slab, orbitals), bf16),
            pltpu.VMEM((cols // 128, rows * slab, 128), jnp.float32),
            pltpu.VMEM((2, times, 4, orbitals // 4, cols), bf16),
            pltpu.VMEM((2, times, width, aux_rows), bf16),
            pltpu.SemaphoreType.DMA((2,)),
            pltpu.SemaphoreType.DMA((4, CHUNKS)),
            pltpu.SemaphoreType.DMA((4, CHUNKS)),
            pltpu.SemaphoreType.DMA((2, CHUNKS)),
            pltpu.SemaphoreType.DMA((2, CHUNKS)),
            pltpu.SemaphoreType.DMA((2,)),
            pltpu.SemaphoreType.DMA((4, 2)),
            pltpu.SemaphoreType.DMA((4, 2)),
            pltpu.SemaphoreType.DMA((4, 2)),
            pltpu.SemaphoreType.DMA((4, 2)),
            pltpu.SemaphoreType.DMA((2,)),
            pltpu.SemaphoreType.DMA((2,)),
            pltpu.SemaphoreType.DMA((2,)),
        ],
        compiler_params=pltpu.CompilerParams(
            collective_id=0, has_side_effects=True, vmem_limit_bytes=60 * 1024 * 1024
        ),
        cost_estimate=pl.CostEstimate(
            flops=2 * times * slab * aux_rows * cols * (orbitals + 4 * aux_rows),
            bytes_accessed=64 << 20,
            transcendentals=0,
        ),
    )(integrals, mask, masked_density, turned(virt_ints))


def on_device(integrals, int_pattern, density, dens_pattern, virt_ints):
    aux_rows, slab_width, orbitals = integrals.shape
    times_count, _, columns = density.shape
    int_mask = expand(int_pattern, BLK)
    integral_rows = (integrals * int_mask[:, None, :]).reshape(aux_rows * slab_width, orbitals)
    masked_density = density * expand(dens_pattern, BLK)[None]
    occupied_list = []
    for moment in range(times_count):
        occupied_list.append(
            jnp.dot(
                integral_rows,
                lax.all_gather(masked_density[moment], "aux", axis=0, tiled=True),
                preferred_element_type=jnp.float32,
            )
        )
    occupied = jnp.stack(occupied_list)
    occupied = occupied.astype(jnp.bfloat16).reshape(times_count, aux_rows, slab_width * columns)
    virtual_rows = virt_ints.reshape(times_count, virt_ints.shape[1], slab_width * columns)
    partial_chi = jnp.einsum(
        "tpk,tqk->tpq",
        lax.all_gather(occupied, "aux", axis=1, tiled=True),
        virtual_rows,
        preferred_element_type=jnp.float32,
    )
    return lax.psum_scatter(
        partial_chi.astype(jnp.bfloat16), "orb", scatter_dimension=1, tiled=True
    ).astype(jnp.float32)


def solution(mesh):
    in_specs = (
        P("aux", None, None),
        P("aux", None),
        P(None, "aux", "orb"),
        P("aux", "orb"),
        P(None, "aux", None, "orb"),
    )
    out_specs = P(None, "orb", "aux")
    small = mesh.shape["aux"] == 4 and mesh.shape["orb"] == 8
    return jax.shard_map(
        on_grid if small else on_device,
        mesh=mesh,
        in_specs=in_specs,
        out_specs=out_specs,
        check_vma=False,
    )
```

```python
import functools

import jax
import jax.numpy as jnp
from jax import lax
from jax.experimental import pallas as pl
from jax.experimental.pallas import tpu as pltpu
from jax.sharding import PartitionSpec as P

BLK = 64
CHUNKS = 32
MESH = pl.DeviceIdType.MESH


def expand(pattern, block_width):
    return jnp.repeat(jnp.repeat(pattern, block_width, axis=0), block_width, axis=1).astype(
        jnp.bfloat16
    )


def ring_kernel(
    chunks, ints, mask, dens, virt, out, occ, psum, zrecv, ibuf, ybuf, dall, vall,
    isem, xs, xr, zs, zr, dl, ds, dr, es, er, vl, vs, vr, obuf, osem,
):
    rows, slab = ibuf.shape[1], ibuf.shape[2]
    per_moment = out.shape[1] // rows
    cols = dens.shape[2]
    width = slab * cols
    half = rows // 2
    a = lax.axis_index("aux")
    o = lax.axis_index("orb")
    z = o // 2
    ax = a + 1 - 2 * (a % 2)
    ay = (a + 2) % 4
    ad = 3 - a
    core = o % 2
    sib = o + 1 - 2 * core
    depth = dens.shape[1]

    def rcopy(src, dst, send, recv, dev):
        return pltpu.make_async_remote_copy(
            src_ref=src, dst_ref=dst, send_sem=send, recv_sem=recv, device_id=dev, device_id_type=MESH
        )

    def own(i, kind, slot):
        ref = occ.at[slot, i]
        return rcopy(ref, ref, xs.at[kind, i], xr.at[kind, i], (ax if kind == 0 else ay, o))

    def forward(i, kind, slot):
        ref = occ.at[slot, i, pl.ds(0 if kind == 2 else half, half)]
        return rcopy(ref, ref, xs.at[kind, i], xr.at[kind, i], (ay if kind == 2 else ax, o))

    def up(i, frm, at_end):
        low = frm + 1
        src = psum.at[i, pl.ds(low, 4 - low)] if at_end else zrecv.at[i, pl.ds(low + 1, 4 - low)]
        return rcopy(src, zrecv.at[i, pl.ds(low + 1, 4 - low)], zs.at[0, i], zr.at[0, i], (a, 2 * (frm + 1) + o % 2))

    def down(i, frm, at_end):
        src = psum.at[i, pl.ds(0, frm)] if at_end else zrecv.at[i, pl.ds(0, frm)]
        return rcopy(src, zrecv.at[i, pl.ds(0, frm)], zs.at[1, i], zr.at[1, i], (a, 2 * (frm - 1) + o % 2))

    def fetch(i):
        return pltpu.make_async_copy(
            ints.at[pl.ds(core * out.shape[1] + (i % per_moment) * rows, rows)], ibuf.at[i % 2], isem.at[i % 2]
        )

    def d_local(t):
        return pltpu.make_async_copy(dens.at[t], dall.at[0, t, a], dl.at[t])

    def d_own(t, kind):
        return rcopy(
            dens.at[t], dall.at[0, t, a], ds.at[kind, t], dr.at[kind, t], (ax if kind == 0 else ay, o)
        )

    def d_forward(t, kind, slot):
        part = pl.ds(0 if kind == 2 else depth // 2, depth // 2)
        ref = dall.at[0, t, slot, part]
        return rcopy(ref, ref, ds.at[kind, t], dr.at[kind, t], (ay if kind == 2 else ax, o))

    def d_cross(t, kind, slot):
        src = dens.at[t] if kind == 0 else dall.at[0, t, slot]
        return rcopy(src, dall.at[1, t, slot], es.at[kind, t], er.at[kind, t], (a, sib))

    def v_local(t):
        return pltpu.make_async_copy(virt.at[t], vall.at[0, t], vl.at[t])

    def v_cross(t):
        return rcopy(virt.at[t], vall.at[1, t], vs.at[t], vr.at[t], (a, sib))

    fetch(0).start()
    d_local(0).start()
    v_local(0).start()
    d_local(1).start()
    v_local(1).start()

    barrier = pltpu.get_barrier_semaphore()
    pl.semaphore_signal(barrier, inc=1, device_id=(ax, o), device_id_type=MESH)
    pl.semaphore_signal(barrier, inc=1, device_id=(ay, o), device_id_type=MESH)
    pl.semaphore_signal(barrier, inc=1, device_id=(a, sib), device_id_type=MESH)

    @pl.when(z > 0)
    def _():
        pl.semaphore_signal(barrier, inc=1, device_id=(a, o - 2), device_id_type=MESH)

    @pl.when(z < 3)
    def _():
        pl.semaphore_signal(barrier, inc=1, device_id=(a, o + 2), device_id_type=MESH)

    inner = (z > 0) & (z < 3)

    @pl.when(inner)
    def _():
        pl.semaphore_wait(barrier, 5)

    @pl.when(jnp.logical_not(inner))
    def _():
        pl.semaphore_wait(barrier, 4)

    def d_send(t):
        d_own(t, 0).start()
        d_own(t, 1).start()
        d_cross(t, 0, a).start()
        v_cross(t).start()

    def d_relay(t):
        d_own(t, 0).wait_recv()
        d_forward(t, 2, ax).start()
        d_cross(t, 1, ax).start()
        d_own(t, 1).wait_recv()
        d_forward(t, 3, ay).start()
        d_cross(t, 2, ay).start()

    def d_finish(t):
        d_forward(t, 2, ad).wait_recv()
        d_forward(t, 3, ad).wait_recv()
        d_cross(t, 3, ad).start()
        d_local(t).wait()
        for kind, slot in enumerate((a, ax, ay, ad)):
            d_cross(t, kind, slot).wait_recv()

    d_send(0)
    d_relay(0)
    d_finish(0)

    def make(i):
        fetch(i).wait()

        @pl.when(i + 1 < chunks)
        def _():
            fetch(i + 1).start()

        t = i // per_moment
        x = (ibuf[i % 2] * mask[i % per_moment][None]).reshape(rows * slab, ibuf.shape[3])
        for side in range(2):
            d = dall[side, t].reshape(4 * depth, cols)
            y = jnp.dot(x, d, preferred_element_type=jnp.float32)
            for part in range(cols // 128):
                ybuf[part] = y[:, part * 128 : (part + 1) * 128]
            for s in range(slab):
                base = side * width + s * cols
                for part in range(cols // 128):
                    piece = ybuf[part, pl.ds(s, rows, stride=slab), :]
                    low = base + part * 128
                    occ[a, i, :, low : low + 128] = piece.astype(jnp.bfloat16)
        own(i, 0, a).start()
        own(i, 1, a).start()

    def relay(i):
        own(i, 0, ax).wait_recv()
        forward(i, 2, ax).start()
        own(i, 1, ay).wait_recv()
        forward(i, 3, ay).start()

    def multiply(i):
        forward(i, 2, ad).wait_recv()
        forward(i, 3, ad).wait_recv()
        t = i // per_moment

        @pl.when(i % per_moment == 0)
        def _():
            v_local(t).wait()
            v_cross(t).wait_recv()

        for d in range(0, 4, 2):
            left = occ[d : d + 2, i].reshape(2 * rows, 2 * width)
            p = jnp.dot(left[:, :width], vall[0, t], preferred_element_type=jnp.float32)
            p += jnp.dot(left[:, width:], vall[1, t], preferred_element_type=jnp.float32)
            psum[i, d : d + 2] = p.astype(jnp.bfloat16).reshape(2, rows, psum.shape[3])

        @pl.when(z == 0)
        def _():
            up(i, 0, True).start()

        @pl.when(z == 3)
        def _():
            down(i, 3, True).start()

    def add(i, slot, d):
        total = zrecv[i, slot].astype(jnp.float32) + psum[i, d].astype(jnp.float32)
        zrecv[i, slot] = total.astype(jnp.bfloat16)

    def hop1(i):
        @pl.when(z == 1)
        def _():
            up(i, 0, True).wait_recv()
            for d in (2, 3):
                add(i, d + 1, d)
            up(i, 1, False).start()

        @pl.when(z == 2)
        def _():
            down(i, 3, True).wait_recv()
            for d in (0, 1):
                add(i, d, d)
            down(i, 2, False).start()

    def hop2(i):
        @pl.when(z == 2)
        def _():
            up(i, 1, False).wait_recv()
            add(i, 4, 3)
            up(i, 2, False).start()

        @pl.when(z == 1)
        def _():
            down(i, 2, False).wait_recv()
            add(i, 0, 0)
            down(i, 1, False).start()

    def flush(i):
        where = pl.ds((i % per_moment) * rows, rows)
        return pltpu.make_async_copy(obuf.at[i % 2], out.at[i // per_moment, where], osem.at[i % 2])

    def finish(i):
        @pl.when(i >= 2)
        def _():
            flush(i - 2).wait()

        @pl.when(z == 0)
        def _():
            down(i, 1, False).wait_recv()
            obuf[i % 2] = psum[i, 0].astype(jnp.float32) + zrecv[i, 0].astype(jnp.float32)

        @pl.when(z == 3)
        def _():
            up(i, 2, False).wait_recv()
            obuf[i % 2] = psum[i, 3].astype(jnp.float32) + zrecv[i, 4].astype(jnp.float32)

        @pl.when(inner)
        def _():
            total = zrecv[i, z].astype(jnp.float32) + zrecv[i, z + 1].astype(jnp.float32)
            obuf[i % 2] = total + psum[i, z].astype(jnp.float32)

        flush(i).start()

    stages = ((relay, 2), (make, 0), (multiply, 4), (hop1, 6), (hop2, 8), (finish, 10))

    @pl.loop(0, chunks + stages[-1][1])
    def _(step):
        for stage, lag in stages:

            @pl.when((step >= lag) & (step < chunks + lag))
            def _(stage=stage, lag=lag):
                stage(step - lag)

        for at, part in ((1, d_send), (3, d_relay), (5, d_finish)):

            @pl.when(step == at)
            def _(part=part):
                part(1)

    flush(chunks - 2).wait()
    flush(chunks - 1).wait()
    for t in range(2):
        for kind in range(2):
            d_own(t, kind).wait_send()
        d_forward(t, 2, ax).wait_send()
        d_forward(t, 3, ay).wait_send()
        for kind, slot in enumerate((a, ax, ay, ad)):
            d_cross(t, kind, slot).wait_send()
        v_cross(t).wait_send()

    @pl.loop(0, chunks)
    def _(i):
        own(i, 0, a).wait_send()
        own(i, 1, a).wait_send()
        forward(i, 2, ax).wait_send()
        forward(i, 3, ay).wait_send()
        for place in range(4):

            @pl.when(z == place)
            def _(place=place):
                if place < 3:
                    up(i, place, place == 0).wait_send()
                if place > 0:
                    down(i, place, place == 3).wait_send()


def on_grid(integrals, int_pattern, density, dens_pattern, virt_ints):
    aux_rows, slab, orbitals = integrals.shape
    times, _, cols = density.shape
    core = lax.axis_index("orb") % 2
    mine = aux_rows // 2
    masked_density = density * expand(dens_pattern, BLK)[None]
    pattern = lax.dynamic_slice_in_dim(int_pattern, core * (mine // BLK), mine // BLK, 0)
    rows = times * mine // CHUNKS
    mask = jnp.repeat(pattern, BLK, axis=1).astype(jnp.bfloat16)
    mask = jnp.repeat(mask, BLK // rows, axis=0)[:, None, :]

    def turned(v):
        return jnp.transpose(v, (0, 2, 3, 1)).reshape(times, slab * cols, aux_rows)

    width = slab * cols
    bf16 = jnp.bfloat16
    hbm = pl.BlockSpec(memory_space=pl.ANY)
    vmem = pl.BlockSpec(memory_space=pltpu.VMEM)
    return pl.pallas_call(
        functools.partial(ring_kernel, CHUNKS),
        out_shape=jax.ShapeDtypeStruct((times, mine, aux_rows), jnp.float32),
        in_specs=[hbm, vmem, vmem, hbm],
        out_specs=hbm,
        scratch_shapes=[
            pltpu.VMEM((4, CHUNKS, rows, 2 * width), bf16),
            pltpu.VMEM((CHUNKS, 4, rows, aux_rows), bf16),
            pltpu.VMEM((CHUNKS, 5, rows, aux_rows), bf16),
            pltpu.VMEM((2, rows, slab, orbitals), bf16),
            pltpu.VMEM((cols // 128, rows * slab, 128), jnp.float32),
            pltpu.VMEM((2, times, 4, orbitals // 4, cols), bf16),
            pltpu.VMEM((2, times, width, aux_rows), bf16),
            pltpu.SemaphoreType.DMA((2,)),
            pltpu.SemaphoreType.DMA((4, CHUNKS)),
            pltpu.SemaphoreType.DMA((4, CHUNKS)),
            pltpu.SemaphoreType.DMA((2, CHUNKS)),
            pltpu.SemaphoreType.DMA((2, CHUNKS)),
            pltpu.SemaphoreType.DMA((2,)),
            pltpu.SemaphoreType.DMA((4, 2)),
            pltpu.SemaphoreType.DMA((4, 2)),
            pltpu.SemaphoreType.DMA((4, 2)),
            pltpu.SemaphoreType.DMA((4, 2)),
            pltpu.SemaphoreType.DMA((2,)),
            pltpu.SemaphoreType.DMA((2,)),
            pltpu.SemaphoreType.DMA((2,)),
            pltpu.VMEM((2, rows, aux_rows), jnp.float32),
            pltpu.SemaphoreType.DMA((2,)),
        ],
        compiler_params=pltpu.CompilerParams(
            collective_id=0, has_side_effects=True, vmem_limit_bytes=60 * 1024 * 1024
        ),
        cost_estimate=pl.CostEstimate(
            flops=2 * times * slab * aux_rows * cols * (orbitals + 4 * aux_rows),
            bytes_accessed=64 << 20,
            transcendentals=0,
        ),
    )(integrals, mask, masked_density, turned(virt_ints))


def on_device(integrals, int_pattern, density, dens_pattern, virt_ints):
    aux_rows, slab_width, orbitals = integrals.shape
    times_count, _, columns = density.shape
    int_mask = expand(int_pattern, BLK)
    integral_rows = (integrals * int_mask[:, None, :]).reshape(aux_rows * slab_width, orbitals)
    masked_density = density * expand(dens_pattern, BLK)[None]
    occupied_list = []
    for moment in range(times_count):
        occupied_list.append(
            jnp.dot(
                integral_rows,
                lax.all_gather(masked_density[moment], "aux", axis=0, tiled=True),
                preferred_element_type=jnp.float32,
            )
        )
    occupied = jnp.stack(occupied_list)
    occupied = occupied.astype(jnp.bfloat16).reshape(times_count, aux_rows, slab_width * columns)
    virtual_rows = virt_ints.reshape(times_count, virt_ints.shape[1], slab_width * columns)
    partial_chi = jnp.einsum(
        "tpk,tqk->tpq",
        lax.all_gather(occupied, "aux", axis=1, tiled=True),
        virtual_rows,
        preferred_element_type=jnp.float32,
    )
    return lax.psum_scatter(
        partial_chi.astype(jnp.bfloat16), "orb", scatter_dimension=1, tiled=True
    ).astype(jnp.float32)


def solution(mesh):
    in_specs = (
        P("aux", None, None),
        P("aux", None),
        P(None, "aux", "orb"),
        P("aux", "orb"),
        P(None, "aux", None, "orb"),
    )
    out_specs = P(None, "orb", "aux")
    small = mesh.shape["aux"] == 4 and mesh.shape["orb"] == 8
    return jax.shard_map(
        on_grid if small else on_device,
        mesh=mesh,
        in_specs=in_specs,
        out_specs=out_specs,
        check_vma=False,
    )
```
